256 devices in a mesh: dp: 32 (over x, z), fsdp: 8 (over y, core).
Axes of the slice: x: 4, y: 4, z: 8, core: 2. Of those that a mesh axis runs over, the one named last changes fastest.
Arguments:
- queries: bfloat16 [256, 64, 2048], P('dp'), may hold values from -6 to 6
- d_out: bfloat16 [256, 64, 2048], P('dp'), may hold values from -24 to 24
- database: bfloat16 [512, 128, 896], P('dp', 'fsdp'), may hold values from -160 to 160
- kv_weight: bfloat16 [4096, 896], P('fsdp'), may hold values from -0.1875 to 0.1875
- gain: bfloat16 [896], P('fsdp'), may hold values from 0.099609375 to 1.8984375
- nbr_owner: int32 [256, 2], replicated, may hold values from 0 to 31, all different within a row; in each aligned block of 8 rows (0 to 7, 8 to 15, ...) at most 2 rows name the same one
- nbr_row: int32 [256, 2], replicated, may hold values from 0 to 15
- nbr_count: int32 [256], P('dp'), may hold values from 1 to 2
Outputs:
- attended: bfloat16 [256, 64, 2048], P('dp', 'fsdp')
- kv_grad: float32 [4096, 896], P(('dp', 'fsdp'))
- gain_grad: float32 [896], replicated
The draws below stay inside these ranges and needn't reach their ends.
Inputs may be any that keep to these rules, and one draw needn't show every extreme that they name: `nbr_owner`: the two owners of a stretch differ. Among the 16 entries of the stretches of one index of dp (aligned blocks of 8 stretches), no owner is named more than 2 times, a bound that some block reaches. A stretch reads its first nbr_count neighbours.
All inputs are finite; a program needn't handle non-finite values.
Results may differ from the reference program's by a relative error of at most 0.02.
Values may be sent and summed in bfloat16 or wider, within the bound.
No kernel may reach another device: no remote copies, remote signals or barrier semaphores. Data moves between devices by JAX's collectives and lax.ppermute only.
A program may use at most 128 MiB of HBM per device.

```python
import math
import jax
import jax.numpy as jnp
import numpy as np
from jax import lax

DE = 896
HS = 128
HEADS = 16
CL = 64
NT = 128
CH_G = 8
DB_DEV = 16
HD = 2048
CAP = 2
CH = 256
NDB = 512
N_DP = 32
N_FSDP = 8


def draw_database(key, part):
    key = jax.random.fold_in(key, 7)
    key_base, key_rows, key_cols = jax.random.split(key, 3)
    row_scale = jnp.exp(jax.random.uniform(key_rows, (NDB, NT, 1), jnp.float32) * jnp.log(10.0))
    col_scale = jnp.exp(jax.random.uniform(key_cols, (1, 1, DE), jnp.float32) * jnp.log(4.0))
    base = jnp.clip(jax.random.normal(key_base, (NDB, NT, DE), jnp.float32), -4.0, 4.0)
    return (base * row_scale * col_scale).astype(jnp.bfloat16)


def place_ends(values, rng, least, largest):
    extent = values.shape
    spot = [jax.random.randint(jax.random.fold_in(rng, axis), (), 0, extent[axis]) for axis in range(len(extent))]
    values = values.at[tuple(spot)].set(least)
    longest = extent.index(max(extent))
    spot[longest] = (spot[longest] + 1) % extent[longest]
    return values.at[tuple(spot)].set(largest)


def steps_of(rng, shape, shards, low, high):
    factor_of, own = 1.0, jax.random.fold_in(rng, 6)
    for axis_at, parts in shards:
        heights = jnp.exp(jax.random.uniform(jax.random.fold_in(own, axis_at), (parts,), jnp.float32, low / len(shards), high / len(shards)))
        factor_of = factor_of * jnp.repeat(heights, shape[axis_at] // parts).reshape([-1 if axis == axis_at else 1 for axis in range(len(shape))])
    return factor_of


def shared_out(stream_key, own, number, rows, count, top, most, lean):
    ranking = jax.random.permutation(stream_key, count)
    packed, usual = portions_of(count, rows * top, most, lean, True), portions_of(count, rows * top, most, lean, False)
    places = jnp.arange(count)

    def named(tallies, rotation):
        used = int((tallies > 0).sum())
        fixed = max(1, used // 4)
        shifted = fixed + (places - fixed + rotation * (used - fixed)) % max(1, count - fixed)
        return jnp.zeros((count,), jnp.int32).at[ranking[jnp.where(places < fixed, places, shifted)]].set(jnp.asarray(tallies, jnp.int32))

    tallies = jnp.where(number % 4 == 0, named(packed, number // 4), named(usual, number - number // 4 - 1))
    mixed = jax.random.permutation(jax.random.fold_in(own, 3), count)
    giver, taker = mixed[0:count // 2 * 2:2], mixed[1:count // 2 * 2:2]
    margin = jnp.minimum(tallies[giver] - 1, most - tallies[taker]) // 2
    margin = jnp.where((giver == ranking[0]) | (taker == ranking[0]) | (tallies[taker] == 0), 0, jnp.maximum(margin, 0))
    shifted = jax.random.randint(jax.random.fold_in(own, 4), (count // 2,), 0, 1 << 20) % (margin + 1)
    tallies = tallies.at[giver].add(-shifted).at[taker].add(shifted)
    members = jnp.searchsorted(jnp.cumsum(tallies), jnp.arange(rows * top), side="right").astype(jnp.int32)
    grid = members.reshape(top, rows).T
    grid = grid[jax.random.permutation(jax.random.fold_in(own, 1), rows)]
    rotation = jax.random.randint(jax.random.fold_in(own, 2), (rows, 1), 0, top)
    return jnp.take_along_axis(grid, (jnp.arange(top)[None, :] + rotation) % top, axis=1)


def portions_of(number_of, total, limit, slope, full):
    portions = [(1 << 20) // math.isqrt(grade ** slope) + 1 for grade in range(1, number_of + 1)]
    largest = limit if full else min(limit, max(-(-total // number_of), total * portions[0] // sum(portions)))
    least = 1 if total - largest >= number_of - 1 else 0
    holding, surplus = [largest] + [least] * (number_of - 1), total - largest - least * (number_of - 1)
    while surplus > 0:
        candidates = [i for i in range(1, number_of) if holding[i] < largest] or [i for i in range(1, number_of) if holding[i] < limit]
        whole, remaining = sum([portions[i] for i in candidates]), surplus
        for i in candidates:
            more = min(limit - holding[i], max(1, remaining * portions[i] // whole), surplus)
            holding[i] = holding[i] + more
            surplus = surplus - more
    return np.array(holding)


def normal_values(own_key, dims, deviation, most, pieces=(), kind=jnp.bfloat16):
    level = steps_of(own_key, dims, pieces, -0.22, 0.18) if pieces else 1.0
    values = jax.random.normal(own_key, dims, jnp.float32) * deviation * level
    return jnp.minimum(jnp.maximum(values, -most), most).astype(kind)


def setup_inputs(seed: int = 0) -> dict:
    streams_of = jax.random.split(jax.random.key(seed), 9)
    queries = normal_values(streams_of[0], (CH, CL, HD), 1.0, 6.0, ((0, 32),))
    d_out = normal_values(streams_of[1], (CH, CL, HD), 4.0, 24.0, ((0, 32),))
    database = draw_database(jax.random.fold_in(streams_of[8], 71), 0)
    kv_weight = normal_values(streams_of[3], (2 * HD, DE), DE ** -0.5, 0.1875, ((0, 8),))
    gain = jnp.clip(1.0 + 0.18 * jax.random.normal(streams_of[4], (DE,), jnp.float32), 0.099609375, 1.8984375).astype(jnp.bfloat16)
    nbr_owner_keys = jax.random.split(jax.random.fold_in(streams_of[5], 1), CH // CH_G)
    nbr_owner_turns = jax.random.permutation(jax.random.fold_in(streams_of[5], 3), CH // CH_G)
    nbr_owner = jax.vmap(lambda own, number: shared_out(jax.random.fold_in(streams_of[5], 2), own, number, CH_G, N_DP, 2, CAP, 1))(nbr_owner_keys, nbr_owner_turns).reshape((CH, 2))
    nbr_row = place_ends(jax.random.randint(streams_of[6], (CH, 2), 0, DB_DEV), jax.random.fold_in(streams_of[6], 1), 0, DB_DEV - 1).astype(jnp.int32)
    nbr_count = place_ends(jax.random.randint(streams_of[7], (CH,), 1, 3), jax.random.fold_in(streams_of[7], 1), 1, 2).astype(jnp.int32)
    return dict(queries=queries, d_out=d_out, database=database, kv_weight=kv_weight, gain=gain, nbr_owner=nbr_owner, nbr_row=nbr_row, nbr_count=nbr_count)


epsilon = 1e-06
clip_rms = 1.0

def settle(array):
    return lax.optimization_barrier(array.astype(jnp.bfloat16)).astype(jnp.float32)

def reference(queries, d_out, database, kv_weight, gain, nbr_owner, nbr_row, nbr_count):
    head_dim = HEADS * HS
    slice_len = NT // N_FSDP
    score_scale = HS ** (-0.5)
    entries = 2 * CH_G
    row_ids = (nbr_owner * DB_DEV + nbr_row).astype(jnp.int32).reshape(N_DP, entries)
    query_groups = queries.reshape(N_DP, CH_G, CL, HEADS, HS)
    grad_groups = d_out.reshape(N_DP, CH_G, CL, HEADS, HS)
    count_groups = nbr_count.reshape(N_DP, CH_G)
    gain_wide = gain.astype(jnp.float32)
    neighbour = jnp.arange(2 * slice_len, dtype=jnp.int32) // slice_len

    def arrange(block):
        block = block.reshape(CH_G, 2, N_FSDP, slice_len, HEADS, HS)
        block = jnp.transpose(block, (0, 2, 1, 3, 4, 5))
        return block.reshape(CH_G, N_FSDP, 2 * slice_len, HEADS, HS).astype(jnp.float32)

    def restore(block):
        block = block.reshape(CH_G, N_FSDP, 2, slice_len, head_dim)
        return jnp.transpose(block, (0, 2, 1, 3, 4)).reshape(entries * NT, head_dim)

    def group_step(carry, inputs):
        weight_sum, gain_sum = carry
        group_ids, query_heads, grad_heads, counts = inputs
        raw_rows = jnp.take(database, group_ids, axis=0).reshape(entries * NT, DE).astype(jnp.float32)
        inv_rms = lax.rsqrt(lax.optimization_barrier(jnp.mean(raw_rows * raw_rows, axis=1, keepdims=True)) + epsilon)
        unit_rows = raw_rows * inv_rms
        normed = (unit_rows * gain_wide).astype(jnp.bfloat16)
        projected = lax.dot_general(normed, kv_weight, (((1,), (1,)), ((), ())), preferred_element_type=jnp.float32).astype(jnp.bfloat16)
        key_heads = arrange(projected[:, :head_dim])
        value_heads = arrange(projected[:, head_dim:])
        query_wide = query_heads.astype(jnp.float32)
        grad_wide = grad_heads.astype(jnp.float32)
        scores = jnp.einsum('cqhd,cfkhd->chqfk', query_wide, key_heads)
        live_mask = (neighbour[None, :] < counts[:, None]).astype(jnp.float32)
        weights_exp = jnp.exp(scores * score_scale) * live_mask[:, None, None, None, :]
        numerator = jnp.einsum('chqfk,cfkhd->fcqhd', settle(weights_exp), value_heads)
        total_numerator = lax.optimization_barrier(jnp.sum(settle(numerator), axis=0))
        total_denominator = lax.optimization_barrier(jnp.sum(settle(lax.optimization_barrier(jnp.sum(weights_exp, axis=4))), axis=3))
        grad_dots = jnp.einsum('cqhd,cfkhd->chqfk', grad_wide, value_heads)
        total_weighted = lax.optimization_barrier(jnp.sum(settle(lax.optimization_barrier(jnp.sum(weights_exp * grad_dots, axis=4))), axis=3))
        row_denominator = jnp.transpose(total_denominator, (0, 2, 1))
        attended = (total_numerator / row_denominator[..., None]).reshape(CH_G, CL, head_dim).astype(jnp.bfloat16)
        probabilities = weights_exp / total_denominator[..., None, None]
        row_delta = total_weighted / total_denominator
        score_grads = probabilities * (grad_dots - row_delta[..., None, None])
        grad_values = jnp.einsum('chqfk,cqhd->cfkhd', settle(probabilities), grad_wide)
        grad_keys = jnp.einsum('chqfk,cqhd->cfkhd', settle(score_grads), query_wide) * score_scale
        grad_proj = jnp.concatenate([restore(grad_keys), restore(grad_values)], axis=1).astype(jnp.bfloat16)
        grad_normed = jnp.dot(grad_proj, kv_weight, preferred_element_type=jnp.float32)
        gain_sum = gain_sum + lax.optimization_barrier(jnp.sum(grad_normed * unit_rows, axis=0))
        weight_sum = weight_sum + lax.dot_general(grad_proj, normed, (((0,), (0,)), ((), ())), preferred_element_type=jnp.float32)
        return ((weight_sum, gain_sum), attended)
    start_state = (jnp.zeros((2 * head_dim, DE), jnp.float32), jnp.zeros((DE,), jnp.float32))
    final_state, attended = lax.scan(group_step, start_state, (row_ids, query_groups, grad_groups, count_groups))
    weight_sum, gain_sum = final_state
    mean_square = (jnp.sum(weight_sum * weight_sum) + jnp.sum(gain_sum * gain_sum)) / (2 * head_dim * DE + DE)
    factor = jnp.minimum(1.0, clip_rms / jnp.sqrt(mean_square + epsilon))
    return (attended.reshape(CH, CL, head_dim), weight_sum * factor, gain_sum * factor)
```

```python
import jax
import jax.numpy as jnp
from jax import lax
from jax.experimental import pallas as pl
from jax.experimental.pallas import tpu as pltpu
from jax.sharding import PartitionSpec as P

HEADS = 16
HEAD = 128
epsilon = 1e-06
clip_rms = 1.0
f32 = jnp.float32
bf16 = jnp.bfloat16


def dot(a, b, ca, cb):
    return lax.dot_general(a, b, (((ca,), (cb,)), ((), ())), preferred_element_type=f32)


def main_kernel(me_ref, count_ref, x_ref, w_ref, gain_ref, q_ref, do_ref, att_ref, out_ref, acc_ref):
    c = pl.program_id(0)
    width = x_ref.shape[-1]
    keys = x_ref.shape[0] * x_ref.shape[1] * x_ref.shape[2]
    scale = HEAD ** (-0.5)
    gain = gain_ref[...].astype(f32)
    x = x_ref[...].reshape(keys, width).astype(f32)
    inv = lax.rsqrt(jnp.mean(x * x, axis=1, keepdims=True) + epsilon)
    normed = ((x * inv) * gain).astype(bf16)
    proj = dot(w_ref[...], normed, 1, 1).astype(bf16)
    lane = lax.broadcasted_iota(jnp.int32, (1, keys), 1)
    live = (((lane // 16) % 2) < count_ref[c]).astype(f32)
    grads = [None] * 4
    for a in range(2):
        cols = slice(a * HEAD, (a + 1) * HEAD)
        key_t = proj[a * HEAD : (a + 1) * HEAD]
        val_t = proj[(2 + a) * HEAD : (3 + a) * HEAD]
        q = q_ref[0, :, cols]
        do = do_ref[0, :, cols]
        weights = jnp.exp(dot(q, key_t, 1, 0) * scale) * live
        inv_den = 1.0 / jnp.sum(weights, axis=1, keepdims=True)
        numerator = dot(weights.astype(bf16), val_t, 1, 1)
        dots = dot(do, val_t, 1, 0)
        delta = jnp.sum(weights * dots, axis=1, keepdims=True) * inv_den
        att_ref[0, :, cols] = (numerator * inv_den).astype(bf16)
        prob = weights * inv_den
        score_grad = prob * (dots - delta)
        grads[a] = dot(q, score_grad.astype(bf16), 0, 0) * scale
        grads[2 + a] = dot(do, prob.astype(bf16), 0, 0)
    grad_t = jnp.concatenate(grads, axis=0).astype(bf16)
    part = dot(grad_t, normed, 1, 0)

    @pl.when(c == 0)
    def _():
        acc_ref[...] = part

    @pl.when(c > 0)
    def _():
        acc_ref[...] += part

    @pl.when(c == pl.num_programs(0) - 1)
    def _():
        blocks = out_ref.shape[0]
        total = acc_ref[...]
        out_ref[:, :, :width] = total.reshape(blocks, 16, width).astype(bf16)
        gain_part = jnp.sum(total * w_ref[...].astype(f32), axis=0, keepdims=True) / gain
        row = lax.broadcasted_iota(jnp.int32, (16, 128), 0)
        out_ref[:, :, width:] = jnp.zeros((blocks, 16, 128), bf16)
        for t in range(width // 128):
            piece = jnp.broadcast_to(gain_part[:, t * 128 : (t + 1) * 128], (16, 128))
            high = piece.astype(bf16).astype(f32)
            tile = jnp.where(row == 0, high, jnp.where(row == 1, piece - high, 0.0)).astype(bf16)
            for quarter in range(4):
                out_ref[4 * t + quarter, :, width:] = tile


def main_call(me, count, tokens, weights, gain, queries, d_out):
    shards, entries, per, width = tokens.shape
    stretches, length, _ = queries.shape
    rows = weights.shape[0]
    blocks = rows // 16
    pair = 2 * HEAD
    grid_spec = pltpu.PrefetchScalarGridSpec(
        num_scalar_prefetch=2,
        grid=(stretches,),
        in_specs=[
            pl.BlockSpec((shards, 2, per, width), lambda c, me, n: (0, c, 0, 0)),
            pl.BlockSpec((rows, width), lambda c, me, n: (0, 0)),
            pl.BlockSpec((1, width), lambda c, me, n: (0, 0)),
            pl.BlockSpec((1, length, pair), lambda c, me, n: (c, 0, me[1])),
            pl.BlockSpec((1, length, pair), lambda c, me, n: (c, 0, me[1])),
        ],
        out_specs=[
            pl.BlockSpec((1, length, pair), lambda c, me, n: (c, 0, 0)),
            pl.BlockSpec((blocks, 16, width + 128), lambda c, me, n: (0, 0, 0)),
        ],
        scratch_shapes=[pltpu.VMEM((rows, width), f32)],
    )
    return pl.pallas_call(
        main_kernel,
        grid_spec=grid_spec,
        out_shape=[
            jax.ShapeDtypeStruct((stretches, length, pair), bf16),
            jax.ShapeDtypeStruct((blocks, 16, width + 128), bf16),
        ],
        compiler_params=pltpu.CompilerParams(vmem_limit_bytes=40 * 1024 * 1024),
        cost_estimate=pl.CostEstimate(flops=4_200_000_000, bytes_accessed=8_000_000, transcendentals=262144),
        name="attend",
    )(me, count, tokens, weights, gain, queries, d_out)


def reduce_kernel(me_ref, in_ref, red_ref, pay_ref):
    width = red_ref.shape[1]
    blocks = in_ref.shape[0]
    total = in_ref[0].astype(f32)
    for i in range(1, blocks):
        total = total + in_ref[i].astype(f32)
    red = total[:, :width]
    red_ref[...] = red
    squares = jnp.sum(jnp.sum(red * red, axis=1, keepdims=True), axis=0, keepdims=True)
    gain = total[0:1, width:] + total[1:2, width:]
    quarter = me_ref[0] % 4
    lane = lax.broadcasted_iota(jnp.int32, (1, 128), 1)
    gain = jnp.where(lane // 32 == quarter, gain, 0.0)
    pay = jnp.where(lane == ((quarter + 1) % 4) * 32, squares, gain)
    pay_ref[...] = jnp.broadcast_to(pay[None], pay_ref.shape)


def final_kernel(pay_ref, red_ref, grad_ref, gain_ref):
    blocks = 32
    pay = pay_ref[...].reshape(blocks, 8, 128)
    rows = jnp.sum(pay, axis=1)
    row = lax.broadcasted_iota(jnp.int32, (blocks, 128), 0)
    lane = lax.broadcasted_iota(jnp.int32, (blocks, 128), 1)
    gains = jnp.where((lane // 32 == row % 4) & (row < 28), rows, 0.0)
    gains = jnp.sum(gains.reshape(8, 4, 128), axis=1)
    squares = jnp.where(lane == ((row + 1) % 4) * 32, rows, 0.0)
    total = jnp.sum(jnp.sum(squares, axis=1, keepdims=True), axis=0, keepdims=True)
    total = total + jnp.sum(jnp.sum(gains * gains, axis=1, keepdims=True), axis=0, keepdims=True)
    count = 4096 * 896 + 896
    factor = jnp.minimum(1.0, clip_rms * lax.rsqrt(total / count + epsilon))
    grad_ref[...] = red_ref[...] * factor
    gain_ref[...] = gains * factor


def on_device(queries, d_out, database, kv_weight, gain, nbr_owner, nbr_row, nbr_count):
    groups = lax.axis_size("dp")
    shards = lax.axis_size("fsdp")
    group = lax.axis_index("dp")
    shard = lax.axis_index("fsdp")
    me = jnp.stack([group, shard]).astype(jnp.int32)
    stretches, length, head_dim = queries.shape
    per, width = database.shape[1:]
    entries = 2 * stretches
    capacity = 2
    owners = nbr_owner.reshape(groups, entries)
    rows = nbr_row.reshape(groups, entries)
    same = owners[:, :, None] == owners[:, None, :]
    earlier = jnp.arange(entries)[None, :] < jnp.arange(entries)[:, None]
    rank = jnp.sum((same & earlier[None]).astype(jnp.int32), axis=2)
    slots = jnp.arange(capacity, dtype=jnp.int32)
    wanted = (owners == group)[:, :, None] & (rank[:, :, None] == slots[None, None, :])
    picked = jnp.sum(jnp.where(wanted, rows[:, :, None], 0), axis=1)
    outgoing = jnp.take(database, picked.reshape(-1), axis=0, mode="clip")
    incoming = lax.all_to_all(
        outgoing.reshape(groups, capacity, per, width), "dp", split_axis=0, concat_axis=0, tiled=True
    )
    my_owner = lax.dynamic_index_in_dim(owners, group, 0, keepdims=False)
    my_rank = lax.dynamic_index_in_dim(rank, group, 0, keepdims=False)
    fetched = jnp.take(
        incoming.reshape(groups * capacity, per, width), my_owner * capacity + my_rank, axis=0, mode="clip"
    )
    half = kv_weight.shape[0] // 2
    high = shard >= shards // 2
    first, second = kv_weight[:half], kv_weight[half:]
    low_half = shards // 2
    pairs_a = [(i, 2 * i) for i in range(low_half)] + [(i + low_half, 2 * i + 1) for i in range(low_half)]
    pairs_b = [(i, 2 * i + 1) for i in range(low_half)] + [(i + low_half, 2 * i) for i in range(low_half)]
    got_a = lax.ppermute(jnp.where(high, second, first), "fsdp", pairs_a)
    got_b = lax.ppermute(jnp.where(high, first, second), "fsdp", pairs_b)
    odd = shard % 2 == 1
    weights = jnp.concatenate([jnp.where(odd, got_b, got_a), jnp.where(odd, got_a, got_b)], axis=0)
    gain_full = lax.all_gather(gain, "fsdp", axis=0, tiled=True).reshape(1, width)
    tokens = lax.all_gather(fetched, "fsdp", axis=0, tiled=False)
    att, blocks = main_call(me, nbr_count, tokens, weights, gain_full, queries, d_out)
    rows_here = length // shards
    att = att.reshape(stretches, shards, rows_here, 2 * HEAD).transpose(1, 0, 2, 3)
    att = lax.all_to_all(att, "fsdp", split_axis=0, concat_axis=0, tiled=True)
    attended = att.transpose(1, 2, 0, 3).reshape(stretches, rows_here, head_dim)
    blocks = lax.all_to_all(blocks, "dp", split_axis=0, concat_axis=0, tiled=True)
    reduced, payload = pl.pallas_call(
        reduce_kernel,
        in_specs=[pl.BlockSpec(memory_space=pltpu.SMEM), pl.BlockSpec(memory_space=pltpu.VMEM)],
        out_specs=[pl.BlockSpec(memory_space=pltpu.VMEM)] * 2,
        out_shape=[
            jax.ShapeDtypeStruct((16, width), f32),
            jax.ShapeDtypeStruct((groups * shards, 1, 128), f32),
        ],
        compiler_params=pltpu.CompilerParams(vmem_limit_bytes=16 * 1024 * 1024),
        name="reduce",
    )(me, blocks)
    pairs = []
    for p in range(groups):
        kv, odd_head, piece = p // 16, (p // 8) % 2, p % 8
        for s in range(shards):
            pairs.append((p * shards + s, (kv * 16 + 2 * s + odd_head) * shards + piece))
    moved = lax.ppermute(reduced, ("dp", "fsdp"), pairs)
    payload = lax.all_to_all(payload, ("dp", "fsdp"), split_axis=0, concat_axis=0, tiled=True)
    kv_grad, gain_grad = pl.pallas_call(
        final_kernel,
        out_shape=[
            jax.ShapeDtypeStruct((16, width), f32),
            jax.ShapeDtypeStruct((8, 128), f32),
        ],
        name="finish",
    )(payload, moved)
    return attended, kv_grad, gain_grad[: width // 128].reshape(width)


def solution(mesh):
    in_specs = (
        P("dp", None, None),
        P("dp", None, None),
        P("dp", "fsdp", None),
        P("fsdp", None),
        P("fsdp"),
        P(),
        P(),
        P("dp"),
    )
    out_specs = (P("dp", "fsdp", None), P(("dp", "fsdp"), None), P())
    return jax.shard_map(
        on_device, mesh=mesh, in_specs=in_specs, out_specs=out_specs, check_vma=False
    )
```

```python
import functools

import jax
import jax.numpy as jnp
from jax import lax
from jax.experimental import pallas as pl
from jax.experimental.pallas import tpu as pltpu
from jax.sharding import PartitionSpec as P

HEADS = 16
HEAD = 128
epsilon = 1e-06
clip_rms = 1.0
f32 = jnp.float32
bf16 = jnp.bfloat16
VMEM = pl.BlockSpec(memory_space=pltpu.VMEM)
SMEM = pl.BlockSpec(memory_space=pltpu.SMEM)
ANY = pl.BlockSpec(memory_space=pl.ANY)
MIB = 1024 * 1024


def dot(a, b, ca, cb):
    return lax.dot_general(a, b, (((ca,), (cb,)), ((), ())), preferred_element_type=f32)


def project(x, weights, gain):
    inv = lax.rsqrt(jnp.mean(x * x, axis=1, keepdims=True) + epsilon)
    normed = ((x * inv) * gain).astype(bf16)
    return normed, dot(normed, weights, 1, 1).astype(bf16)


def project_kernel(a_ref, b_ref, w_ref, gain_ref, normed_ref, proj_ref):
    gain = gain_ref[...].astype(f32)
    weights = w_ref[...]
    stretches = normed_ref.shape[0]
    per = a_ref.shape[0] // stretches
    for i, ref in enumerate((a_ref, b_ref)):
        normed, proj = project(ref[...].astype(f32), weights, gain)
        for c in range(stretches):
            normed_ref[c, i * per : (i + 1) * per, :] = normed[c * per : (c + 1) * per]
            proj_ref[c, i * per : (i + 1) * per, :] = proj[c * per : (c + 1) * per]


def project_call(first, second, weights, gain, stretches):
    rows, width = weights.shape
    per = 2 * first.shape[0] // stretches
    return pl.pallas_call(
        project_kernel,
        in_specs=[VMEM] * 4,
        out_specs=[VMEM] * 2,
        out_shape=[
            jax.ShapeDtypeStruct((stretches, per, width), bf16),
            jax.ShapeDtypeStruct((stretches, per, rows), bf16),
        ],
        compiler_params=pltpu.CompilerParams(vmem_limit_bytes=14 * MIB),
        cost_estimate=pl.CostEstimate(flops=500_000_000, bytes_accessed=4_000_000, transcendentals=512),
        name="project",
    )(first, second, weights, gain)


def main_kernel(blocks_before, me_ref, count_ref, *refs):
    normed_in, refs = refs[:blocks_before], refs[blocks_before:]
    proj_in, refs = refs[:blocks_before], refs[blocks_before:]
    a_ref, b_ref, w_ref, gain_ref, q_hbm, do_hbm, att_ref, out_ref, *refs = refs
    q_ref, do_ref, normed_ref, proj_ref, grad_ref, sems = refs
    stretches, keys, width = normed_ref.shape
    pair = 2 * HEAD
    scale = HEAD ** (-0.5)
    start = pl.multiple_of(me_ref[1] * pair, pair)
    part = normed_in[0].shape[1]
    copies = [
        pltpu.make_async_copy(q_hbm.at[:, :, pl.ds(start, pair)], q_ref, sems.at[0]),
        pltpu.make_async_copy(do_hbm.at[:, :, pl.ds(start, pair)], do_ref, sems.at[1]),
    ]
    late = []
    for i in range(blocks_before):
        here = slice(i * part, (i + 1) * part)
        copies.append(pltpu.make_async_copy(proj_in[i], proj_ref.at[:, here, :], sems.at[2 + 2 * i]))
        late.append(pltpu.make_async_copy(normed_in[i], normed_ref.at[:, here, :], sems.at[3 + 2 * i]))
    for copy in copies + late:
        copy.start()
    gain = gain_ref[...].astype(f32)
    weights_here = w_ref[...]
    per = a_ref.shape[0] // stretches
    for i, ref in enumerate((a_ref, b_ref)):
        normed, proj = project(ref[...].astype(f32), weights_here, gain)
        at = blocks_before * part + i * per
        for c in range(stretches):
            normed_ref[c, at : at + per, :] = normed[c * per : (c + 1) * per]
            proj_ref[c, at : at + per, :] = proj[c * per : (c + 1) * per]
    for copy in copies:
        copy.wait()
    lane = lax.broadcasted_iota(jnp.int32, (1, keys), 1)
    neighbour = (lane // (per // 2)) % 2
    for c in range(stretches):
        live = (neighbour < count_ref[c]).astype(f32)
        for a in range(2):
            cols = slice(a * HEAD, (a + 1) * HEAD)
            key = proj_ref[c, :, a * HEAD : (a + 1) * HEAD]
            val = proj_ref[c, :, (2 + a) * HEAD : (3 + a) * HEAD]
            q = q_ref[c, :, cols]
            do = do_ref[c, :, cols]
            weights = jnp.exp(dot(q, key, 1, 1) * scale) * live
            inv_den = 1.0 / jnp.sum(weights, axis=1, keepdims=True)
            numerator = dot(weights.astype(bf16), val, 1, 0)
            dots = dot(do, val, 1, 1)
            delta = jnp.sum(weights * dots, axis=1, keepdims=True) * inv_den
            att_ref[c, :, cols] = (numerator * inv_den).astype(bf16)
            prob = weights * inv_den
            score_grad = prob * (dots - delta)
            here = slice(c * keys, (c + 1) * keys)
            grad_ref[a * HEAD : (a + 1) * HEAD, here] = (
                dot(q, score_grad.astype(bf16), 0, 0) * scale
            ).astype(bf16)
            grad_ref[(2 + a) * HEAD : (3 + a) * HEAD, here] = dot(do, prob.astype(bf16), 0, 0).astype(bf16)
    for copy in late:
        copy.wait()
    blocks = out_ref.shape[0]
    out_ref[:, :, width:] = jnp.zeros((blocks, 16, 128), bf16)
    gain_part = jnp.zeros((1, width), f32)
    normed_all = normed_ref[...].reshape(stretches * keys, width)
    for a in range(4):
        here = slice(a * HEAD, (a + 1) * HEAD)
        raw = dot(grad_ref[here, :], normed_all, 1, 0)
        out_ref[a * 8 : (a + 1) * 8, :, :width] = raw.reshape(8, 16, width).astype(bf16)
        gain_part = gain_part + jnp.sum(raw * w_ref[here, :].astype(f32), axis=0, keepdims=True)
    gain_part = gain_part / gain
    row = lax.broadcasted_iota(jnp.int32, (16, 128), 0)
    for t in range(width // 128):
        piece = jnp.broadcast_to(gain_part[:, t * 128 : (t + 1) * 128], (16, 128))
        high = piece.astype(bf16).astype(f32)
        tile = jnp.where(row == 0, high, jnp.where(row == 1, piece - high, 0.0)).astype(bf16)
        for quarter in range(4):
            out_ref[4 * t + quarter, :, width:] = tile


def main_call(me, count, normed, proj, first, second, weights, gain, queries, d_out):
    stretches, length, _ = queries.shape
    rows, width = weights.shape
    keys = normed[0].shape[1] * (len(normed) + 1)
    blocks = rows // 16
    pair = 2 * HEAD
    return pl.pallas_call(
        functools.partial(main_kernel, len(normed)),
        in_specs=[SMEM] * 2 + [ANY] * (2 * len(normed)) + [VMEM] * 4 + [ANY] * 2,
        out_specs=[VMEM] * 2,
        out_shape=[
            jax.ShapeDtypeStruct((stretches, length, pair), bf16),
            jax.ShapeDtypeStruct((blocks, 16, width + 128), bf16),
        ],
        scratch_shapes=[
            pltpu.VMEM((stretches, length, pair), bf16),
            pltpu.VMEM((stretches, length, pair), bf16),
            pltpu.VMEM((stretches, keys, width), bf16),
            pltpu.VMEM((stretches, keys, rows), bf16),
            pltpu.VMEM((rows, stretches * keys), bf16),
            pltpu.SemaphoreType.DMA((2 + 2 * len(normed),)),
        ],
        compiler_params=pltpu.CompilerParams(vmem_limit_bytes=24 * MIB),
        cost_estimate=pl.CostEstimate(flops=4_200_000_000, bytes_accessed=8_000_000, transcendentals=262144),
        name="attend",
    )(me, count, *normed, *proj, first, second, weights, gain, queries, d_out)


def pick_kernel(at_ref, in_ref, w_ref, gain_ref, out_ref, sems):
    count = at_ref.shape[0]
    per = in_ref.shape[1]
    copies = [
        pltpu.make_async_copy(in_ref.at[at_ref[i]], out_ref.at[pl.ds(i * per, per)], sems.at[i])
        for i in range(count)
    ]
    for copy in copies:
        copy.start()
    for copy in copies:
        copy.wait()


def pick_call(at, incoming, weights, gain):
    _, per, width = incoming.shape
    return pl.pallas_call(
        pick_kernel,
        in_specs=[SMEM, ANY, ANY, ANY],
        out_specs=VMEM,
        out_shape=jax.ShapeDtypeStruct((at.shape[0] * per, width), bf16),
        scratch_shapes=[pltpu.SemaphoreType.DMA((at.shape[0],))],
        compiler_params=pltpu.CompilerParams(vmem_limit_bytes=4 * MIB),
        name="pick",
    )(at, incoming, weights, gain)


def reduce_kernel(me_ref, in_ref, red_ref, pay_ref):
    width = red_ref.shape[1]
    blocks = in_ref.shape[0]
    total = in_ref[0].astype(f32)
    for i in range(1, blocks):
        total = total + in_ref[i].astype(f32)
    red = total[:, :width]
    red_ref[...] = red
    squares = jnp.sum(jnp.sum(red * red, axis=1, keepdims=True), axis=0, keepdims=True)
    gain = total[0:1, width:] + total[1:2, width:]
    quarter = me_ref[0] % 4
    lane = lax.broadcasted_iota(jnp.int32, (1, 128), 1)
    gain = jnp.where(lane // 32 == quarter, gain, 0.0)
    pay = jnp.where(lane == ((quarter + 1) % 4) * 32, squares, gain)
    pay_ref[...] = jnp.broadcast_to(pay[None], pay_ref.shape)


def final_kernel(pay_ref, red_ref, grad_ref, gain_ref):
    blocks = 32
    pay = pay_ref[...].reshape(blocks, 8, 128)
    rows = jnp.sum(pay, axis=1)
    row = lax.broadcasted_iota(jnp.int32, (blocks, 128), 0)
    lane = lax.broadcasted_iota(jnp.int32, (blocks, 128), 1)
    gains = jnp.where((lane // 32 == row % 4) & (row < 28), rows, 0.0)
    gains = jnp.sum(gains.reshape(8, 4, 128), axis=1)
    squares = jnp.where(lane == ((row + 1) % 4) * 32, rows, 0.0)
    total = jnp.sum(jnp.sum(squares, axis=1, keepdims=True), axis=0, keepdims=True)
    total = total + jnp.sum(jnp.sum(gains * gains, axis=1, keepdims=True), axis=0, keepdims=True)
    count = 4096 * 896 + 896
    factor = jnp.minimum(1.0, clip_rms * lax.rsqrt(total / count + epsilon))
    grad_ref[...] = red_ref[...] * factor
    gains = gains * factor
    for t in range(gain_ref.shape[0] // 128):
        gain_ref[t * 128 : (t + 1) * 128] = gains[t]


def on_device(queries, d_out, database, kv_weight, gain, nbr_owner, nbr_row, nbr_count):
    groups = lax.axis_size("dp")
    shards = lax.axis_size("fsdp")
    group = lax.axis_index("dp")
    shard = lax.axis_index("fsdp")
    me = jnp.stack([group, shard]).astype(jnp.int32)
    stretches, length, head_dim = queries.shape
    per, width = database.shape[1:]
    entries = 2 * stretches
    capacity = 2
    at_group = jnp.arange(groups * stretches) // stretches
    place = jnp.arange(groups * stretches) % stretches * 2
    order = jnp.stack([place, place + 1])
    keys = order * 16 + nbr_row.T
    wanted = (nbr_owner.T == group)[None] & (at_group[None, None] == jnp.arange(groups)[:, None, None])
    first = jnp.min(jnp.where(wanted, keys[None], 256), axis=(1, 2))
    last = jnp.max(jnp.where(wanted, keys[None], 0), axis=(1, 2))
    picked = jnp.stack([first, last], axis=1) % 16
    outgoing = jnp.take(database, picked.reshape(-1), axis=0, mode="clip")
    incoming = lax.all_to_all(
        outgoing.reshape(groups, capacity, per, width), "dp", split_axis=0, concat_axis=0, tiled=True
    )
    my_owner = lax.dynamic_slice_in_dim(nbr_owner, group * stretches, stretches, 0).reshape(entries)
    earlier = jnp.arange(entries)[None, :] < jnp.arange(entries)[:, None]
    my_rank = jnp.any((my_owner[None, :] == my_owner[:, None]) & earlier, axis=1)
    half = kv_weight.shape[0] // 2
    high = shard >= shards // 2
    first, second = kv_weight[:half], kv_weight[half:]
    low_half = shards // 2
    pairs_a = [(i, 2 * i) for i in range(low_half)] + [(i + low_half, 2 * i + 1) for i in range(low_half)]
    pairs_b = [(i, 2 * i + 1) for i in range(low_half)] + [(i + low_half, 2 * i) for i in range(low_half)]
    got_a = lax.ppermute(jnp.where(high, second, first), "fsdp", pairs_a)
    got_b = lax.ppermute(jnp.where(high, first, second), "fsdp", pairs_b)
    odd = shard % 2 == 1
    weights = jnp.concatenate([jnp.where(odd, got_b, got_a), jnp.where(odd, got_a, got_b)], axis=0)
    lanes = jnp.arange(width) // gain.shape[0]
    gain_full = jnp.where(lanes == shard, jnp.tile(gain, shards), 0)[None]
    for step in (1, 2, 4):
        gain_full = gain_full + lax.ppermute(gain_full, "fsdp", [(i, i ^ step) for i in range(shards)])
    at = (my_owner * capacity + my_rank.astype(jnp.int32)).astype(jnp.int32)
    own = pick_call(at, incoming.reshape(groups * capacity, per, width), weights, gain_full)
    ring = [(i, (i + (2 if i % 2 == 0 else -2)) % shards) for i in range(shards)]
    swap = [(i, i ^ 1) for i in range(shards)]
    move = lambda block, pairs: lax.ppermute(block, "fsdp", pairs)
    near = move(own, ring)
    other = move(own, swap)
    near_b = move(other, ring)
    far = move(near, ring)
    pieces = [(own, other), (near, move(near, swap)), (near_b, move(near_b, swap))]
    done = [project_call(x, y, weights, gain_full, stretches) for x, y in pieces]
    far, done[0], done[1] = lax.optimization_barrier((far, done[0], done[1]))
    att, blocks = main_call(
        me,
        nbr_count,
        [n for n, _ in done],
        [p for _, p in done],
        far,
        move(far, swap),
        weights,
        gain_full,
        queries,
        d_out,
    )
    rows_here = length // shards
    att = att.reshape(stretches, shards, rows_here, 2 * HEAD)
    attended = jnp.zeros((stretches, rows_here, head_dim), bf16)
    for step in range(shards):
        peer = shard ^ step
        piece = lax.dynamic_index_in_dim(att, peer, 1, keepdims=False)
        if step:
            piece = lax.ppermute(piece, "fsdp", [(i, i ^ step) for i in range(shards)])
        attended = lax.dynamic_update_slice_in_dim(attended, piece, peer * 2 * HEAD, 2)
    blocks = lax.all_to_all(blocks, "dp", split_axis=0, concat_axis=0, tiled=True)
    reduced, payload = pl.pallas_call(
        reduce_kernel,
        in_specs=[SMEM, VMEM],
        out_specs=[VMEM] * 2,
        out_shape=[
            jax.ShapeDtypeStruct((16, width), f32),
            jax.ShapeDtypeStruct((groups * shards, 1, 128), f32),
        ],
        compiler_params=pltpu.CompilerParams(vmem_limit_bytes=4 * MIB),
        name="reduce",
    )(me, blocks)
    pairs = []
    for p in range(groups):
        kv, odd_head, piece = p // 16, (p // 8) % 2, p % 8
        for s in range(shards):
            pairs.append((p * shards + s, (kv * 16 + 2 * s + odd_head) * shards + piece))
    moved = lax.ppermute(reduced, ("dp", "fsdp"), pairs)
    payload = lax.all_to_all(payload, ("dp", "fsdp"), split_axis=0, concat_axis=0, tiled=True)
    kv_grad, gain_grad = pl.pallas_call(
        final_kernel,
        out_shape=[
            jax.ShapeDtypeStruct((16, width), f32),
            jax.ShapeDtypeStruct((width,), f32),
        ],
        compiler_params=pltpu.CompilerParams(vmem_limit_bytes=4 * MIB),
        name="finish",
    )(payload, moved)
    return attended, kv_grad, gain_grad


def solution(mesh):
    in_specs = (
        P("dp", None, None),
        P("dp", None, None),
        P("dp", "fsdp", None),
        P("fsdp", None),
        P("fsdp"),
        P(),
        P(),
        P("dp"),
    )
    out_specs = (P("dp", "fsdp", None), P(("dp", "fsdp"), None), P())
    return jax.shard_map(
        on_device, mesh=mesh, in_specs=in_specs, out_specs=out_specs, check_vma=False
    )
```

```python
import functools

import jax
import jax.numpy as jnp
from jax import lax
from jax.experimental import pallas as pl
from jax.experimental.pallas import tpu as pltpu
from jax.sharding import PartitionSpec as P

HEADS = 16
HEAD = 128
epsilon = 1e-06
clip_rms = 1.0
f32 = jnp.float32
bf16 = jnp.bfloat16
VMEM = pl.BlockSpec(memory_space=pltpu.VMEM)
SMEM = pl.BlockSpec(memory_space=pltpu.SMEM)
ANY = pl.BlockSpec(memory_space=pl.ANY)
MIB = 1024 * 1024


def dot(a, b, ca, cb):
    return lax.dot_general(a, b, (((ca,), (cb,)), ((), ())), preferred_element_type=f32)


def project(x, weights, gain):
    inv = lax.rsqrt(jnp.mean(x * x, axis=1, keepdims=True) + epsilon)
    normed = ((x * inv) * gain).astype(bf16)
    return normed, dot(normed, weights, 1, 1).astype(bf16)


def project_kernel(a_ref, b_ref, w_ref, gain_ref, normed_ref, proj_ref):
    gain = gain_ref[...].astype(f32)
    weights = w_ref[...]
    stretches = normed_ref.shape[0]
    per = a_ref.shape[0] // stretches
    for i, ref in enumerate((a_ref, b_ref)):
        normed, proj = project(ref[...].astype(f32), weights, gain)
        for c in range(stretches):
            normed_ref[c, i * per : (i + 1) * per, :] = normed[c * per : (c + 1) * per]
            proj_ref[c, i * per : (i + 1) * per, :] = proj[c * per : (c + 1) * per]


def project_call(first, second, weights, gain, stretches):
    rows, width = weights.shape
    per = 2 * first.shape[0] // stretches
    return pl.pallas_call(
        project_kernel,
        in_specs=[VMEM] * 4,
        out_specs=[VMEM] * 2,
        out_shape=[
            jax.ShapeDtypeStruct((stretches, per, width), bf16),
            jax.ShapeDtypeStruct((stretches, per, rows), bf16),
        ],
        compiler_params=pltpu.CompilerParams(vmem_limit_bytes=14 * MIB),
        cost_estimate=pl.CostEstimate(flops=500_000_000, bytes_accessed=4_000_000, transcendentals=512),
        name="project",
    )(first, second, weights, gain)


def main_kernel(blocks_before, me_ref, count_ref, *refs):
    normed_in, refs = refs[:blocks_before], refs[blocks_before:]
    proj_in, refs = refs[:blocks_before], refs[blocks_before:]
    a_ref, b_ref, w_ref, gain_ref, q_hbm, do_hbm, att_ref, out_ref, part_ref, *refs = refs
    q_ref, do_ref, normed_ref, proj_ref, grad_ref, stage_ref, in_sems, out_sems = refs
    stretches, keys, width = normed_ref.shape
    scale = HEAD ** (-0.5)
    part = normed_in[0].shape[1]
    pair = 2 * HEAD
    start = pl.multiple_of(me_ref[1] * pair, pair)
    early = [
        pltpu.make_async_copy(q_hbm.at[:, :, pl.ds(start, pair)], q_ref, in_sems.at[blocks_before]),
        pltpu.make_async_copy(do_hbm.at[:, :, pl.ds(start, pair)], do_ref, in_sems.at[blocks_before + 1]),
    ]
    copies = [
        pltpu.make_async_copy(ref, normed_ref.at[:, i * part : (i + 1) * part, :], in_sems.at[i])
        for i, ref in enumerate(normed_in)
    ]
    for copy in early + copies:
        copy.start()
    gain = gain_ref[...].astype(f32)
    weights_here = w_ref[...]
    per = a_ref.shape[0] // stretches
    for i, ref in enumerate((a_ref, b_ref)):
        normed, proj = project(ref[...].astype(f32), weights_here, gain)
        at = blocks_before * part + i * per
        for c in range(stretches):
            normed_ref[c, at : at + per, :] = normed[c * per : (c + 1) * per]
            proj_ref[c, i * per : (i + 1) * per, :] = proj[c * per : (c + 1) * per]
    for copy in early:
        copy.wait()
    proj_all = (*proj_in, proj_ref)
    lane = lax.broadcasted_iota(jnp.int32, (1, keys), 1)
    neighbour = (lane // (per // 2)) % 2
    for c in range(stretches):
        live = (neighbour < count_ref[c]).astype(f32)
        for a in range(2):
            cols = slice(a * HEAD, (a + 1) * HEAD)
            val_cols = slice((2 + a) * HEAD, (3 + a) * HEAD)
            key = jnp.concatenate([ref[c, :, cols] for ref in proj_all], axis=0)
            val = jnp.concatenate([ref[c, :, val_cols] for ref in proj_all], axis=0)
            q = q_ref[c, :, cols]
            do = do_ref[c, :, cols]
            weights = jnp.exp(dot(q, key, 1, 1) * scale) * live
            inv_den = 1.0 / jnp.sum(weights, axis=1, keepdims=True)
            numerator = dot(weights.astype(bf16), val, 1, 0)
            dots = dot(do, val, 1, 1)
            delta = jnp.sum(weights * dots, axis=1, keepdims=True) * inv_den
            att_ref[c, :, cols] = (numerator * inv_den).astype(bf16)
            prob = weights * inv_den
            score_grad = prob * (dots - delta)
            here = slice(c * keys, (c + 1) * keys)
            grad_ref[cols, here] = (dot(q, score_grad.astype(bf16), 0, 0) * scale).astype(bf16)
            grad_ref[val_cols, here] = dot(do, prob.astype(bf16), 0, 0).astype(bf16)
    for copy in copies:
        copy.wait()
    gain_part = jnp.zeros((1, width), f32)
    normed_all = normed_ref[...].reshape(stretches * keys, width)
    sends = []
    for a in range(4):
        here = slice(a * HEAD, (a + 1) * HEAD)
        raw = dot(grad_ref[here, :], normed_all, 1, 0)
        stage_ref[a] = raw.reshape(8, 16, width).astype(bf16)
        sends.append(
            pltpu.make_async_copy(stage_ref.at[a], out_ref.at[pl.ds(a * 8, 8)], out_sems.at[a])
        )
        sends[a].start()
        gain_part = gain_part + jnp.sum(raw * w_ref[here, :].astype(f32), axis=0, keepdims=True)
    part_ref[...] = gain_part / gain
    for send in sends:
        send.wait()


def main_call(me, count, normed, proj, first, second, weights, gain, queries, d_out):
    stretches, length, _ = queries.shape
    pair = 2 * HEAD
    rows, width = weights.shape
    before = len(normed)
    part = normed[0].shape[1]
    keys = part * (before + 1)
    blocks = rows // 16
    return pl.pallas_call(
        functools.partial(main_kernel, before),
        in_specs=[SMEM] * 2 + [ANY] * before + [VMEM] * (before + 4) + [ANY] * 2,
        out_specs=[VMEM, pl.BlockSpec(memory_space=pltpu.HBM), VMEM],
        out_shape=[
            jax.ShapeDtypeStruct((stretches, length, pair), bf16),
            jax.ShapeDtypeStruct((blocks, 16, width), bf16),
            jax.ShapeDtypeStruct((1, width), f32),
        ],
        scratch_shapes=[
            pltpu.VMEM((stretches, length, pair), bf16),
            pltpu.VMEM((stretches, length, pair), bf16),
            pltpu.VMEM((stretches, keys, width), bf16),
            pltpu.VMEM((stretches, part, rows), bf16),
            pltpu.VMEM((rows, stretches * keys), bf16),
            pltpu.VMEM((4, 8, 16, width), bf16),
            pltpu.SemaphoreType.DMA((before + 2,)),
            pltpu.SemaphoreType.DMA((4,)),
        ],
        compiler_params=pltpu.CompilerParams(vmem_limit_bytes=20 * MIB),
        cost_estimate=pl.CostEstimate(flops=4_200_000_000, bytes_accessed=8_000_000, transcendentals=262144),
        name="attend",
    )(me, count, *normed, *proj, first, second, weights, gain, queries, d_out)


def pick_kernel(at_ref, in_ref, w_ref, gain_ref, out_ref, sems):
    count = at_ref.shape[0]
    per = in_ref.shape[1]
    copies = [
        pltpu.make_async_copy(in_ref.at[at_ref[i]], out_ref.at[pl.ds(i * per, per)], sems.at[i])
        for i in range(count)
    ]
    for copy in copies:
        copy.start()
    for copy in copies:
        copy.wait()


def pick_call(at, incoming, weights, gain):
    _, per, width = incoming.shape
    return pl.pallas_call(
        pick_kernel,
        in_specs=[SMEM, ANY, ANY, ANY],
        out_specs=VMEM,
        out_shape=jax.ShapeDtypeStruct((at.shape[0] * per, width), bf16),
        scratch_shapes=[pltpu.SemaphoreType.DMA((at.shape[0],))],
        compiler_params=pltpu.CompilerParams(vmem_limit_bytes=4 * MIB),
        name="pick",
    )(at, incoming, weights, gain)


def reduce_kernel(me_ref, in_ref, gain_ref, red_ref, pay_ref):
    total = in_ref[0].astype(f32)
    for i in range(1, in_ref.shape[0]):
        total = total + in_ref[i].astype(f32)
    red_ref[...] = total
    squares = jnp.sum(jnp.sum(total * total, axis=1, keepdims=True), axis=0, keepdims=True)
    lane = lax.broadcasted_iota(jnp.int32, (8, 128), 1)
    pay = jnp.broadcast_to(squares, (8, 128))
    for t in range(gain_ref.shape[1] // 128):
        tile = jnp.broadcast_to(gain_ref[:, t * 128 : (t + 1) * 128], (8, 128))
        turn = lax.rem(16 * t + 128 - 16 * me_ref[1], 128)
        pay = jnp.where(lane // 16 == t, pltpu.roll(tile, turn, 1), pay)
    pay_ref[...] = jnp.broadcast_to(pay[0:1][None], pay_ref.shape)


def final_kernel(count, pay_ref, red_ref, grad_ref, gain_ref):
    rows = jnp.sum(pay_ref[...].reshape(-1, 8, 128), axis=0)
    row = lax.broadcasted_iota(jnp.int32, (8, 128), 0)
    lane = lax.broadcasted_iota(jnp.int32, (8, 128), 1)
    turned = [rows] + [pltpu.roll(rows, 16 * d, 1) for d in range(1, 8)]
    gains = []
    for t in range(gain_ref.shape[0] // 128):
        tile = jnp.zeros((8, 128), f32)
        for d in range(8):
            tile = jnp.where((row == lane // 16) & (row == (t + d) % 8), turned[d], tile)
        gains.append(jnp.sum(tile, axis=0, keepdims=True))
    squares = jnp.where(lane == 112, rows, 0.0)
    for tile in gains:
        squares = squares + jnp.where(row == 0, jnp.broadcast_to(tile * tile, (8, 128)), 0.0)
    total = jnp.sum(jnp.sum(squares, axis=1, keepdims=True), axis=0, keepdims=True)
    factor = jnp.minimum(1.0, clip_rms * lax.rsqrt(total / count + epsilon))
    grad_ref[...] = red_ref[...] * factor
    for t, tile in enumerate(gains):
        gain_ref[t * 128 : (t + 1) * 128] = (tile * factor)[0]


def on_device(queries, d_out, database, kv_weight, gain, nbr_owner, nbr_row, nbr_count):
    groups = lax.axis_size("dp")
    shards = lax.axis_size("fsdp")
    group = lax.axis_index("dp")
    shard = lax.axis_index("fsdp")
    me = jnp.stack([group, shard]).astype(jnp.int32)
    stretches, length, head_dim = queries.shape
    per, width = database.shape[1:]
    entries = 2 * stretches
    capacity = 2
    at_group = jnp.arange(groups * stretches) // stretches
    place = jnp.arange(groups * stretches) % stretches * 2
    order = jnp.stack([place, place + 1])
    keys = order * 16 + nbr_row.T
    wanted = (nbr_owner.T == group)[None] & (at_group[None, None] == jnp.arange(groups)[:, None, None])
    first = jnp.min(jnp.where(wanted, keys[None], 256), axis=(1, 2))
    last = jnp.max(jnp.where(wanted, keys[None], 0), axis=(1, 2))
    picked = jnp.stack([first, last], axis=1) % 16
    outgoing = jnp.take(database, picked.reshape(-1), axis=0, mode="clip")
    incoming = lax.all_to_all(
        outgoing.reshape(groups, capacity, per, width), "dp", split_axis=0, concat_axis=0, tiled=True
    )
    my_owner = lax.dynamic_slice_in_dim(nbr_owner, group * stretches, stretches, 0).reshape(entries)
    earlier = jnp.arange(entries)[None, :] < jnp.arange(entries)[:, None]
    my_rank = jnp.any((my_owner[None, :] == my_owner[:, None]) & earlier, axis=1)
    half = kv_weight.shape[0] // 2
    high = shard >= shards // 2
    first, second = kv_weight[:half], kv_weight[half:]
    low_half = shards // 2
    pairs_a = [(i, 2 * i) for i in range(low_half)] + [(i + low_half, 2 * i + 1) for i in range(low_half)]
    pairs_b = [(i, 2 * i + 1) for i in range(low_half)] + [(i + low_half, 2 * i) for i in range(low_half)]
    got_a = lax.ppermute(jnp.where(high, second, first), "fsdp", pairs_a)
    got_b = lax.ppermute(jnp.where(high, first, second), "fsdp", pairs_b)
    odd = shard % 2 == 1
    weights = jnp.concatenate([jnp.where(odd, got_b, got_a), jnp.where(odd, got_a, got_b)], axis=0)
    lanes = jnp.arange(width) // gain.shape[0]
    gain_full = jnp.where(lanes == shard, jnp.tile(gain, shards), 0)[None]
    for step in (1, 2, 4):
        gain_full = gain_full + lax.ppermute(gain_full, "fsdp", [(i, i ^ step) for i in range(shards)])
    at = (my_owner * capacity + my_rank.astype(jnp.int32)).astype(jnp.int32)
    own = pick_call(at, incoming.reshape(groups * capacity, per, width), weights, gain_full)
    ring = [(i, (i + (2 if i % 2 == 0 else -2)) % shards) for i in range(shards)]
    swap = [(i, i ^ 1) for i in range(shards)]
    move = lambda block, pairs: lax.ppermute(block, "fsdp", pairs)
    near = move(own, ring)
    other = move(own, swap)
    near_b = move(other, ring)
    far = move(near, ring)
    pieces = [(own, other), (near, move(near, swap)), (near_b, move(near_b, swap))]
    done = [project_call(x, y, weights, gain_full, stretches) for x, y in pieces]
    far, done[0], done[1] = lax.optimization_barrier((far, done[0], done[1]))
    att, blocks, gain_part = main_call(
        me,
        nbr_count,
        [n for n, _ in done],
        [p for _, p in done],
        far,
        move(far, swap),
        weights,
        gain_full,
        queries,
        d_out,
    )
    for step in (1, 2, 4):
        gain_part = gain_part + lax.ppermute(gain_part, "fsdp", [(i, i ^ step) for i in range(shards)])
    rows_here = length // shards
    att = att.reshape(stretches, shards, rows_here, 2 * HEAD)
    attended = jnp.zeros((stretches, rows_here, head_dim), bf16)
    for step in range(shards):
        peer = shard ^ step
        piece = lax.dynamic_index_in_dim(att, peer, 1, keepdims=False)
        if step:
            piece = lax.ppermute(piece, "fsdp", [(i, i ^ step) for i in range(shards)])
        attended = lax.dynamic_update_slice_in_dim(attended, piece, peer * 2 * HEAD, 2)
    blocks = lax.all_to_all(blocks, "dp", split_axis=0, concat_axis=0, tiled=True)
    reduced, payload = pl.pallas_call(
        reduce_kernel,
        in_specs=[SMEM, VMEM, VMEM],
        out_specs=[VMEM] * 2,
        out_shape=[
            jax.ShapeDtypeStruct((16, width), f32),
            jax.ShapeDtypeStruct((groups * shards, 1, 128), f32),
        ],
        compiler_params=pltpu.CompilerParams(vmem_limit_bytes=4 * MIB),
        name="reduce",
    )(me, blocks, gain_part)
    pairs = []
    for p in range(groups):
        kv, odd_head, piece = p // 16, (p // 8) % 2, p % 8
        for s in range(shards):
            pairs.append((p * shards + s, (kv * 16 + 2 * s + odd_head) * shards + piece))
    moved = lax.ppermute(reduced, ("dp", "fsdp"), pairs)
    payload = lax.all_to_all(payload, ("dp", "fsdp"), split_axis=0, concat_axis=0, tiled=True)
    kv_grad, gain_grad = pl.pallas_call(
        functools.partial(final_kernel, groups * 16 * shards * width + width),
        out_shape=[
            jax.ShapeDtypeStruct((16, width), f32),
            jax.ShapeDtypeStruct((width,), f32),
        ],
        compiler_params=pltpu.CompilerParams(vmem_limit_bytes=4 * MIB),
        name="finish",
    )(payload, moved)
    return attended, kv_grad, gain_grad


def solution(mesh):
    in_specs = (
        P("dp", None, None),
        P("dp", None, None),
        P("dp", "fsdp", None),
        P("fsdp", None),
        P("fsdp"),
        P(),
        P(),
        P("dp"),
    )
    out_specs = (P("dp", "fsdp", None), P(("dp", "fsdp"), None), P())
    return jax.shard_map(
        on_device, mesh=mesh, in_specs=in_specs, out_specs=out_specs, check_vma=False
    )
```

```python
import functools

import jax
import jax.numpy as jnp
from jax import lax
from jax.experimental import pallas as pl
from jax.experimental.pallas import tpu as pltpu
from jax.sharding import PartitionSpec as P

HEADS = 16
HEAD = 128
epsilon = 1e-06
clip_rms = 1.0
f32 = jnp.float32
bf16 = jnp.bfloat16
VMEM = pl.BlockSpec(memory_space=pltpu.VMEM)
SMEM = pl.BlockSpec(memory_space=pltpu.SMEM)
ANY = pl.BlockSpec(memory_space=pl.ANY)
MIB = 1024 * 1024


def dot(a, b, ca, cb):
    return lax.dot_general(a, b, (((ca,), (cb,)), ((), ())), preferred_element_type=f32)


def project(x, weights, gain):
    inv = lax.rsqrt(jnp.mean(x * x, axis=1, keepdims=True) + epsilon)
    normed = ((x * inv) * gain).astype(bf16)
    return normed, dot(normed, weights, 1, 1).astype(bf16)


def project_kernel(a_ref, b_ref, w_ref, gain_ref, normed_ref, proj_ref):
    gain = gain_ref[...].astype(f32)
    weights = w_ref[...]
    stretches = normed_ref.shape[0]
    per = a_ref.shape[0] // stretches
    for i, ref in enumerate((a_ref, b_ref)):
        normed, proj = project(ref[...].astype(f32), weights, gain)
        for c in range(stretches):
            normed_ref[c, i * per : (i + 1) * per, :] = normed[c * per : (c + 1) * per]
            proj_ref[c, i * per : (i + 1) * per, :] = proj[c * per : (c + 1) * per]


def project_call(first, second, weights, gain, stretches):
    rows, width = weights.shape
    per = 2 * first.shape[0] // stretches
    return pl.pallas_call(
        project_kernel,
        in_specs=[VMEM] * 4,
        out_specs=[VMEM] * 2,
        out_shape=[
            jax.ShapeDtypeStruct((stretches, per, width), bf16),
            jax.ShapeDtypeStruct((stretches, per, rows), bf16),
        ],
        compiler_params=pltpu.CompilerParams(vmem_limit_bytes=14 * MIB),
        cost_estimate=pl.CostEstimate(flops=500_000_000, bytes_accessed=4_000_000, transcendentals=512),
        name="project",
    )(first, second, weights, gain)


def main_kernel(blocks_before, me_ref, count_ref, *refs):
    normed_in, refs = refs[:blocks_before], refs[blocks_before:]
    proj_in, refs = refs[:blocks_before], refs[blocks_before:]
    a_ref, b_ref, w_ref, gain_ref, q_hbm, do_hbm, att_ref, keep_ref, send_ref, part_ref, *refs = refs
    q_ref, do_ref, normed_ref, proj_ref, grad_ref, in_sems = refs
    stretches, keys, width = normed_ref.shape
    scale = HEAD ** (-0.5)
    part = normed_in[0].shape[1]
    pair = 2 * HEAD
    start = pl.multiple_of(me_ref[1] * pair, pair)
    early = [
        pltpu.make_async_copy(q_hbm.at[:, :, pl.ds(start, pair)], q_ref, in_sems.at[blocks_before]),
        pltpu.make_async_copy(do_hbm.at[:, :, pl.ds(start, pair)], do_ref, in_sems.at[blocks_before + 1]),
    ]
    copies = [
        pltpu.make_async_copy(ref, normed_ref.at[:, i * part : (i + 1) * part, :], in_sems.at[i])
        for i, ref in enumerate(normed_in)
    ]
    for copy in early + copies:
        copy.start()
    gain = gain_ref[...].astype(f32)
    weights_here = w_ref[...]
    per = a_ref.shape[0] // stretches
    for i, ref in enumerate((a_ref, b_ref)):
        normed, proj = project(ref[...].astype(f32), weights_here, gain)
        at = blocks_before * part + i * per
        for c in range(stretches):
            normed_ref[c, at : at + per, :] = normed[c * per : (c + 1) * per]
            proj_ref[c, i * per : (i + 1) * per, :] = proj[c * per : (c + 1) * per]
    for copy in early:
        copy.wait()
    proj_all = (*proj_in, proj_ref)
    lane = lax.broadcasted_iota(jnp.int32, (1, keys), 1)
    neighbour = (lane // (per // 2)) % 2
    for c in range(stretches):
        live = (neighbour < count_ref[c]).astype(f32)
        for a in range(2):
            cols = slice(a * HEAD, (a + 1) * HEAD)
            val_cols = slice((2 + a) * HEAD, (3 + a) * HEAD)
            key = jnp.concatenate([ref[c, :, cols] for ref in proj_all], axis=0)
            val = jnp.concatenate([ref[c, :, val_cols] for ref in proj_all], axis=0)
            q = q_ref[c, :, cols]
            do = do_ref[c, :, cols]
            weights = jnp.exp(dot(q, key, 1, 1) * scale) * live
            inv_den = 1.0 / jnp.sum(weights, axis=1, keepdims=True)
            numerator = dot(weights.astype(bf16), val, 1, 0)
            dots = dot(do, val, 1, 1)
            delta = jnp.sum(weights * dots, axis=1, keepdims=True) * inv_den
            att_ref[c, :, cols] = (numerator * inv_den).astype(bf16)
            prob = weights * inv_den
            score_grad = prob * (dots - delta)
            here = slice(c * keys, (c + 1) * keys)
            grad_ref[cols, here] = (dot(q, score_grad.astype(bf16), 0, 0) * scale).astype(bf16)
            grad_ref[val_cols, here] = dot(do, prob.astype(bf16), 0, 0).astype(bf16)
    for copy in copies:
        copy.wait()
    gain_part = jnp.zeros((1, width), f32)
    normed_all = normed_ref[...].reshape(stretches * keys, width)
    odd = lax.rem(me_ref[0] // 8, 2)
    for i in range(4):
        at = pl.multiple_of(((i // 2 + odd) % 2 * 2 + i % 2) * HEAD, HEAD)
        raw = dot(grad_ref[pl.ds(at, HEAD), :], normed_all, 1, 0)
        out_ref = keep_ref if i < 2 else send_ref
        out_ref[i % 2 * 8 : (i % 2 + 1) * 8] = raw.reshape(8, 16, width).astype(bf16)
        gain_part = gain_part + jnp.sum(raw * w_ref[pl.ds(at, HEAD), :].astype(f32), axis=0, keepdims=True)
    part_ref[...] = gain_part / gain


def main_call(me, count, normed, proj, first, second, weights, gain, queries, d_out):
    stretches, length, _ = queries.shape
    pair = 2 * HEAD
    rows, width = weights.shape
    before = len(normed)
    part = normed[0].shape[1]
    keys = part * (before + 1)
    blocks = rows // 16
    return pl.pallas_call(
        functools.partial(main_kernel, before),
        in_specs=[SMEM] * 2 + [ANY] * before + [VMEM] * (before + 4) + [ANY] * 2,
        out_specs=[VMEM] * 4,
        out_shape=[
            jax.ShapeDtypeStruct((stretches, length, pair), bf16),
            jax.ShapeDtypeStruct((blocks // 2, 16, width), bf16),
            jax.ShapeDtypeStruct((blocks // 2, 16, width), bf16),
            jax.ShapeDtypeStruct((1, width), f32),
        ],
        scratch_shapes=[
            pltpu.VMEM((stretches, length, pair), bf16),
            pltpu.VMEM((stretches, length, pair), bf16),
            pltpu.VMEM((stretches, keys, width), bf16),
            pltpu.VMEM((stretches, part, rows), bf16),
            pltpu.VMEM((rows, stretches * keys), bf16),
            pltpu.SemaphoreType.DMA((before + 2,)),
        ],
        compiler_params=pltpu.CompilerParams(vmem_limit_bytes=20 * MIB),
        cost_estimate=pl.CostEstimate(flops=4_200_000_000, bytes_accessed=8_000_000, transcendentals=262144),
        name="attend",
    )(me, count, *normed, *proj, first, second, weights, gain, queries, d_out)


def wanted_kernel(me_ref, owner_ref, row_ref, out_ref):
    stretches = 8
    shape = owner_ref.shape
    lane = lax.broadcasted_iota(jnp.int32, shape, 1)
    which = lax.broadcasted_iota(jnp.int32, shape, 0)
    key = ((lane % stretches) * 2 + which) * 16 + row_ref[...]
    mine = owner_ref[...] == me_ref[0]
    low = jnp.where(mine, key, 256)
    high = jnp.where(mine, key, 0)
    low = jnp.minimum(low[0:1], low[1:2])
    high = jnp.maximum(high[0:1], high[1:2])
    for step in (1, 2, 4):
        low = jnp.minimum(low, pltpu.roll(low, shape[1] - step, 1))
        high = jnp.maximum(high, pltpu.roll(high, shape[1] - step, 1))
    both = jnp.concatenate([low % 16, high % 16], axis=0).astype(f32)
    source = lax.broadcasted_iota(jnp.int32, (shape[1], 128), 0)
    slot = lax.broadcasted_iota(jnp.int32, (shape[1], 128), 1)
    chosen = dot(both, (source == slot // 2 * stretches).astype(f32), 1, 0)
    slot = lax.broadcasted_iota(jnp.int32, (1, 128), 1)
    out_ref[...] = jnp.where(slot % 2 == 0, chosen[0:1], chosen[1:2]).astype(jnp.int32)


def wanted_call(me, owner, row):
    return pl.pallas_call(
        wanted_kernel,
        in_specs=[SMEM, VMEM, VMEM],
        out_specs=VMEM,
        out_shape=jax.ShapeDtypeStruct((1, 128), jnp.int32),
        compiler_params=pltpu.CompilerParams(vmem_limit_bytes=4 * MIB),
        name="wanted",
    )(me, owner, row)


def pick_kernel(at_ref, in_ref, w_ref, gain_ref, out_ref, sems):
    count = at_ref.shape[0]
    per = in_ref.shape[1]
    copies = [
        pltpu.make_async_copy(in_ref.at[at_ref[i]], out_ref.at[pl.ds(i * per, per)], sems.at[i])
        for i in range(count)
    ]
    for copy in copies:
        copy.start()
    for copy in copies:
        copy.wait()


def pick_call(at, incoming, weights, gain):
    _, per, width = incoming.shape
    return pl.pallas_call(
        pick_kernel,
        in_specs=[SMEM, ANY, ANY, ANY],
        out_specs=VMEM,
        out_shape=jax.ShapeDtypeStruct((at.shape[0] * per, width), bf16),
        scratch_shapes=[pltpu.SemaphoreType.DMA((at.shape[0],))],
        compiler_params=pltpu.CompilerParams(vmem_limit_bytes=4 * MIB),
        name="pick",
    )(at, incoming, weights, gain)


def add_kernel(a_ref, b_ref, out_ref):
    for i in range(out_ref.shape[0]):
        out_ref[i] = (a_ref[i].astype(f32) + b_ref[i].astype(f32)).astype(bf16)


def reduce_kernel(me_ref, in_ref, gain_ref, red_ref, pay_ref):
    total = in_ref[0].astype(f32)
    for i in range(1, in_ref.shape[0]):
        total = total + in_ref[i].astype(f32)
    red_ref[...] = total
    squares = jnp.sum(jnp.sum(total * total, axis=1, keepdims=True), axis=0, keepdims=True)
    lane = lax.broadcasted_iota(jnp.int32, (8, 128), 1)
    pay = jnp.broadcast_to(squares, (8, 128))
    for t in range(gain_ref.shape[1] // 128):
        tile = jnp.broadcast_to(gain_ref[:, t * 128 : (t + 1) * 128], (8, 128))
        turn = lax.rem(16 * t + 128 - 16 * me_ref[1], 128)
        pay = jnp.where(lane // 16 == t, pltpu.roll(tile, turn, 1), pay)
    pay_ref[...] = jnp.broadcast_to(pay[0:1][None], pay_ref.shape)


def final_kernel(count, pay_ref, red_ref, grad_ref, gain_ref):
    rows = jnp.sum(pay_ref[...].reshape(-1, 8, 128), axis=0)
    row = lax.broadcasted_iota(jnp.int32, (8, 128), 0)
    lane = lax.broadcasted_iota(jnp.int32, (8, 128), 1)
    turned = [rows] + [pltpu.roll(rows, 16 * d, 1) for d in range(1, 8)]
    gains = []
    for t in range(gain_ref.shape[0] // 128):
        tile = jnp.zeros((8, 128), f32)
        for d in range(8):
            tile = jnp.where((row == lane // 16) & (row == (t + d) % 8), turned[d], tile)
        gains.append(jnp.sum(tile, axis=0, keepdims=True))
    squares = jnp.where(lane == 112, rows, 0.0)
    for tile in gains:
        squares = squares + jnp.where(row == 0, jnp.broadcast_to(tile * tile, (8, 128)), 0.0)
    total = jnp.sum(jnp.sum(squares, axis=1, keepdims=True), axis=0, keepdims=True)
    factor = jnp.minimum(1.0, clip_rms * lax.rsqrt(total / count + epsilon))
    grad_ref[...] = red_ref[...] * factor
    for t, tile in enumerate(gains):
        gain_ref[t * 128 : (t + 1) * 128] = (tile * factor)[0]


def on_device(queries, d_out, database, kv_weight, gain, nbr_owner, nbr_row, nbr_count):
    groups = lax.axis_size("dp")
    shards = lax.axis_size("fsdp")
    group = lax.axis_index("dp")
    shard = lax.axis_index("fsdp")
    me = jnp.stack([group, shard]).astype(jnp.int32)
    stretches, length, head_dim = queries.shape
    per, width = database.shape[1:]
    entries = 2 * stretches
    capacity = 2
    picked = wanted_call(me, nbr_owner.T, nbr_row.T)[0, : groups * capacity]
    outgoing = jnp.take(database, picked, axis=0, mode="clip")
    incoming = lax.all_to_all(
        outgoing.reshape(groups, capacity, per, width), "dp", split_axis=0, concat_axis=0, tiled=True
    )
    my_owner = lax.dynamic_slice_in_dim(nbr_owner, group * stretches, stretches, 0).reshape(entries)
    earlier = jnp.arange(entries)[None, :] < jnp.arange(entries)[:, None]
    my_rank = jnp.any((my_owner[None, :] == my_owner[:, None]) & earlier, axis=1)
    half = kv_weight.shape[0] // 2
    high = shard >= shards // 2
    first, second = kv_weight[:half], kv_weight[half:]
    low_half = shards // 2
    pairs_a = [(i, 2 * i) for i in range(low_half)] + [(i + low_half, 2 * i + 1) for i in range(low_half)]
    pairs_b = [(i, 2 * i + 1) for i in range(low_half)] + [(i + low_half, 2 * i) for i in range(low_half)]
    got_a = lax.ppermute(jnp.where(high, second, first), "fsdp", pairs_a)
    got_b = lax.ppermute(jnp.where(high, first, second), "fsdp", pairs_b)
    odd = shard % 2 == 1
    weights = jnp.concatenate([jnp.where(odd, got_b, got_a), jnp.where(odd, got_a, got_b)], axis=0)
    lanes = jnp.arange(width) // gain.shape[0]
    gain_full = jnp.where(lanes == shard, jnp.tile(gain, shards), 0)[None]
    for step in (1, 2, 4):
        gain_full = gain_full + lax.ppermute(gain_full, "fsdp", [(i, i ^ step) for i in range(shards)])
    at = (my_owner * capacity + my_rank.astype(jnp.int32)).astype(jnp.int32)
    own = pick_call(at, incoming.reshape(groups * capacity, per, width), weights, gain_full)
    ring = [(i, (i + (2 if i % 2 == 0 else -2)) % shards) for i in range(shards)]
    swap = [(i, i ^ 1) for i in range(shards)]
    move = lambda block, pairs: lax.ppermute(block, "fsdp", pairs)
    near = move(own, ring)
    other = move(own, swap)
    near_b = move(other, ring)
    far = move(near, ring)
    pieces = [(own, other), (near, move(near, swap)), (near_b, move(near_b, swap))]
    done = [project_call(x, y, weights, gain_full, stretches) for x, y in pieces]
    far, done[0], done[1] = lax.optimization_barrier((far, done[0], done[1]))
    att, keep, send, gain_part = main_call(
        me,
        nbr_count,
        [n for n, _ in done],
        [p for _, p in done],
        far,
        move(far, swap),
        weights,
        gain_full,
        queries,
        d_out,
    )
    for step in (1, 2, 4):
        gain_part = gain_part + lax.ppermute(gain_part, "fsdp", [(i, i ^ step) for i in range(shards)])
    rows_here = length // shards
    att = att.reshape(stretches, shards, rows_here, 2 * HEAD)
    attended = jnp.zeros((stretches, rows_here, head_dim), bf16)
    for step in range(shards):
        peer = shard ^ step
        piece = lax.dynamic_index_in_dim(att, peer, 1, keepdims=False)
        if step:
            piece = lax.ppermute(piece, "fsdp", [(i, i ^ step) for i in range(shards)])
        attended = lax.dynamic_update_slice_in_dim(attended, piece, peer * 2 * HEAD, 2)
    depth = 8
    line = groups // depth
    mates = []
    for p in range(groups):
        for i in range(shards):
            x, z = p // depth, p % depth
            mate = x ^ 1 if i % 2 == 0 else (x - 1) % line if x % 2 == 0 else (x + 1) % line
            mates.append((p * shards + i, (mate * depth + z) * shards + i))
    got = lax.ppermute(send, ("dp", "fsdp"), mates)
    got, gain_part = lax.optimization_barrier((got, gain_part))
    blocks = pl.pallas_call(
        add_kernel,
        in_specs=[VMEM] * 2,
        out_specs=VMEM,
        out_shape=jax.ShapeDtypeStruct(keep.shape, bf16),
        compiler_params=pltpu.CompilerParams(vmem_limit_bytes=4 * MIB),
        name="pairs",
    )(keep, got)
    same = [[x * depth + z for x in range(odd, line, 2) for z in range(depth)] for odd in range(2)]
    blocks = lax.all_to_all(blocks, "dp", 0, 0, tiled=True, axis_index_groups=same)
    reduced, payload = pl.pallas_call(
        reduce_kernel,
        in_specs=[SMEM, VMEM, VMEM],
        out_specs=[VMEM] * 2,
        out_shape=[
            jax.ShapeDtypeStruct((16, width), f32),
            jax.ShapeDtypeStruct((groups * shards, 1, 128), f32),
        ],
        compiler_params=pltpu.CompilerParams(vmem_limit_bytes=4 * MIB),
        name="reduce",
    )(me, blocks, gain_part)
    pairs = []
    for p in range(groups):
        odd_head, kv, piece = p // 16, (p // 8) % 2, p % 8
        for s in range(shards):
            pairs.append((p * shards + s, (kv * 16 + 2 * s + odd_head) * shards + piece))
    moved = lax.ppermute(reduced, ("dp", "fsdp"), pairs)
    payload = lax.all_to_all(payload, ("dp", "fsdp"), split_axis=0, concat_axis=0, tiled=True)
    kv_grad, gain_grad = pl.pallas_call(
        functools.partial(final_kernel, groups * 16 * shards * width + width),
        out_shape=[
            jax.ShapeDtypeStruct((16, width), f32),
            jax.ShapeDtypeStruct((width,), f32),
        ],
        compiler_params=pltpu.CompilerParams(vmem_limit_bytes=4 * MIB),
        name="finish",
    )(payload, moved)
    return attended, kv_grad, gain_grad


def solution(mesh):
    in_specs = (
        P("dp", None, None),
        P("dp", None, None),
        P("dp", "fsdp", None),
        P("fsdp", None),
        P("fsdp"),
        P(),
        P(),
        P("dp"),
    )
    out_specs = (P("dp", "fsdp", None), P(("dp", "fsdp"), None), P())
    return jax.shard_map(
        on_device, mesh=mesh, in_specs=in_specs, out_specs=out_specs, check_vma=False
    )
```
